256 devices in a mesh: row: 64 (over z, x, core), col: 4 (over y).
Axes of the slice: x: 4, y: 4, z: 8, core: 2. Of those that a mesh axis runs over, the one named last changes fastest.
Arguments:
- slab: bfloat16 [180224, 8192], P('row', 'col'), may hold values from -70 to 70, as said below
- test_matrix: bfloat16 [8192, 128], P('col'), may hold values from -0.0625 to 0.0625
Outputs:
- basis: bfloat16 [180224, 128], P('row')
- projected: float32 [8192, 128], P(('col', 'row'))
The draws below stay inside these ranges and needn't reach their ends.
Inputs may be any that keep to these rules, and one draw needn't show every extreme that they name: Every entry is finite, and the sketch (slab times test_matrix) has full column rank.
All inputs are finite; a program needn't handle non-finite values.
Results may differ from the reference program's by a relative error of at most 0.004.
Values may be sent and summed in bfloat16 or wider, within the bound.
No kernel may reach another device: no remote copies, remote signals or barrier semaphores. Data moves between devices by JAX's collectives and lax.ppermute only.
A program may use at most 128 MiB of HBM per device.

```python
import math
import jax
import jax.numpy as jnp
from jax import lax

W = 8192
K = 128
NROWS = 180224


def draw_slab(key, part):
    key = jax.random.fold_in(key, 11)
    keys = jax.random.split(key, 3)
    row_scale = jnp.exp(jax.random.uniform(keys[1], (NROWS, 1), jnp.float32) * math.log(10.0)) / math.sqrt(10.0)
    col_scale = jnp.exp(jax.random.uniform(keys[2], (1, W), jnp.float32) * math.log(10.0)) / math.sqrt(10.0)
    ramp = jnp.sqrt(1.0 + 2.0 * jnp.arange(NROWS, dtype=jnp.float32)[:, None] / (NROWS - 1))
    base = jnp.clip(jax.random.normal(keys[0], (NROWS, W), jnp.float32), -4.0, 4.0)
    return (base * row_scale * ramp * col_scale).astype(jnp.bfloat16)


def block_scale(key, shape, cuts, low, high):
    factor_of, own = 1.0, jax.random.fold_in(key, 6)
    for position, parts in cuts:
        heights = jnp.exp(jax.random.uniform(jax.random.fold_in(own, position), (parts,), jnp.float32, low / len(cuts), high / len(cuts)))
        factor_of = factor_of * jnp.repeat(heights, shape[position] // parts).reshape([-1 if axis == position else 1 for axis in range(len(shape))])
    return factor_of


def centred(stream_key, shape, scale, bound, cuts=(), kind=jnp.bfloat16):
    values = scale * jax.random.normal(stream_key, shape, jnp.float32)
    if cuts:
        values = values * block_scale(stream_key, shape, cuts, -0.22, 0.18)
    return jnp.clip(values, -bound, bound).astype(kind)


def setup_inputs(seed: int = 0) -> dict:
    key_list = jax.random.split(jax.random.key(seed), 3)
    return {
        "slab": draw_slab(jax.random.fold_in(key_list[2], 71), 0),
        "test_matrix": centred(key_list[1], (W, K), W ** -0.5, 0.0625, ((0, 4),)),
    }


def reference(slab, test_matrix):
    sketched = jnp.dot(slab.astype(jnp.float32), test_matrix.astype(jnp.float32), preferred_element_type=jnp.float32)
    gram = jnp.dot(sketched.T.astype(jnp.float32), sketched.astype(jnp.float32), precision=lax.Precision.HIGHEST, preferred_element_type=jnp.float32) / NROWS
    lower = jnp.linalg.cholesky(gram)
    identity = jnp.eye(K, dtype=jnp.float32)
    inverse = jax.scipy.linalg.solve_triangular(lower, identity, lower=True).T
    basis = jnp.dot(sketched.astype(jnp.float32), inverse.astype(jnp.float32), precision=lax.Precision.HIGHEST, preferred_element_type=jnp.float32).astype(jnp.bfloat16)
    projected = lax.dot_general(slab.astype(jnp.float32), basis.astype(jnp.float32), (((0,), (0,)), ((), ())), preferred_element_type=jnp.float32)
    projected = projected / jnp.sqrt(jnp.float32(NROWS))
    return (basis, projected)
```

```python
import jax
import jax.numpy as jnp
from jax import lax
from jax.sharding import PartitionSpec as P

Z, X, C, Y = 8, 4, 2, 4


def row_of(z, x, c):
    return ((z % Z) * X + x % X) * C + c % C


def row_shift(value, dz, dx, dc):
    pairs = [
        (row_of(z, x, c), row_of(z + dz, x + dx, c + dc))
        for z in range(Z)
        for x in range(X)
        for c in range(C)
    ]
    return lax.ppermute(value, "row", pairs)


def col_shift(value, dy):
    return lax.ppermute(value, "col", [(y, (y + dy) % Y) for y in range(Y)])


def body(slab, test_matrix):
    rows, columns = slab.shape
    width = test_matrix.shape[1]
    total_rows = rows * lax.axis_size("row")
    quarter = rows // Y
    me_y = lax.axis_index("col")
    row = lax.axis_index("row")
    me_c, me_x = row % C, (row // C) % X

    def part(shift):
        start = ((me_y + shift) % Y) * quarter
        block = lax.dynamic_slice_in_dim(slab, start, quarter, 0)
        return jnp.dot(block, test_matrix, preferred_element_type=jnp.float32)

    received = [col_shift(part(dy), dy) for dy in (2, 1, 3)]
    own = part(0)
    for piece in received:
        own = own + piece
    own = own.astype(jnp.bfloat16)

    pieces = [own] + [col_shift(own, dy) for dy in (1, 2, 3)]
    sketch = jnp.zeros((rows, width), jnp.bfloat16)
    for dy, piece in enumerate(pieces):
        sketch = lax.dynamic_update_slice_in_dim(sketch, piece, ((me_y - dy) % Y) * quarter, 0)

    dims = (((0,), (0,)), ((), ()))
    product = lax.dot_general(slab, sketch, dims, preferred_element_type=jnp.float32)
    gram = lax.dot_general(sketch, sketch, dims, preferred_element_type=jnp.float32)

    half = width // C
    product = product.reshape(Z, X, C, 32, width)
    gram = gram.reshape(C, half, width)

    def pick(array, index, axis):
        return lax.dynamic_index_in_dim(array, index, axis, keepdims=False)

    def joined(a, b):
        return jnp.concatenate([a.reshape(-1, width), b], 0)

    state = joined(pick(product, me_c, 2), pick(gram, me_c, 0))
    state = state + row_shift(joined(pick(product, 1 - me_c, 2), pick(gram, 1 - me_c, 0)), 0, 0, 1)

    product, gram = state[:-half].reshape(Z, X, 32, width), state[-half:]
    state = joined(pick(product, me_x, 1), gram)
    for dx in (2, 1, 3):
        state = state + row_shift(joined(pick(product, (me_x + dx) % X, 1), gram), 0, dx, 0)

    product, gram = state[:-half].reshape(Z, 32, width), state[-half:]
    packed = jnp.concatenate([product, jnp.broadcast_to(gram[None], (Z, half, width))], 1)
    groups = [[row_of(z, x, c) for z in range(Z)] for x in range(X) for c in range(C)]
    packed = lax.all_to_all(packed, "row", 0, 0, axis_index_groups=groups)
    state = jnp.sum(packed, 0)
    product, gram = state[:32], state[32:]
    other = row_shift(gram, 0, 0, 1)
    gram = jnp.where(me_c == 0, jnp.concatenate([gram, other], 0), jnp.concatenate([other, gram], 0))

    lower = jnp.linalg.cholesky(gram / total_rows)
    identity = jnp.eye(width, dtype=jnp.float32)
    inverse = jax.scipy.linalg.solve_triangular(lower, identity, lower=True).T
    high = inverse.astype(jnp.bfloat16)
    low = (inverse - high.astype(jnp.float32)).astype(jnp.bfloat16)
    basis = jnp.dot(sketch, high, preferred_element_type=jnp.float32)
    basis = basis + jnp.dot(sketch, low, preferred_element_type=jnp.float32)
    factor = 1.0 / jnp.sqrt(jnp.float32(total_rows))
    projected = jnp.dot(product, inverse * factor, precision=lax.Precision.HIGHEST)
    return (basis.astype(jnp.bfloat16), projected)


def solution(mesh):
    placed = (P("row", "col"), P("col", None))
    return jax.shard_map(
        body,
        mesh=mesh,
        in_specs=placed,
        out_specs=(P("row", None), P(("col", "row"), None)),
        check_vma=False,
    )
```

```python
import jax
import jax.numpy as jnp
from jax import lax
from jax.experimental import pallas as pl
from jax.experimental.pallas import tpu as pltpu
from jax.sharding import PartitionSpec as P

Z, X, C, Y = 8, 4, 2, 4
F32, BF16, F16 = jnp.float32, jnp.bfloat16, jnp.float16
VMEM = pl.BlockSpec(memory_space=pltpu.VMEM)
SMEM = pl.BlockSpec(memory_space=pltpu.SMEM)
ANY = pl.BlockSpec(memory_space=pl.ANY)
MIB = 2**20
TAIL = 16


def row_of(z, x, c):
    return ((z % Z) * X + x % X) * C + c % C


def row_shift(value, dz, dx, dc):
    pairs = [
        (row_of(z, x, c), row_of(z + dz, x + dx, c + dc))
        for z in range(Z)
        for x in range(X)
        for c in range(C)
    ]
    return lax.ppermute(value, "row", pairs)


def col_shift(value, dy):
    return lax.ppermute(value, "col", [(y, (y + dy) % Y) for y in range(Y)])


def scaled(value):
    top = jnp.max(jnp.abs(value), axis=0, keepdims=True)
    exponent = jnp.floor(jnp.log2(jnp.maximum(top, 1e-30)))
    return value * jnp.exp2(-exponent), jnp.broadcast_to(exponent, (TAIL, value.shape[1]))


def unscaled(ref):
    rows = ref.shape[0] - TAIL
    return ref[0:rows, :] * jnp.exp2(ref[rows : rows + 1, :])


def sketch_kernel(me, slab, test, remote, own, held, sems):
    quarter = own.shape[0]
    parts = 2
    tile = quarter // parts
    starts = []
    for shift in (2, 1, 3, 0):
        base = lax.rem(me[0] + shift, Y) * quarter
        starts += [pl.multiple_of(base + t * tile, 16) for t in range(parts)]
    copies = [
        pltpu.make_async_copy(slab.at[pl.ds(s, tile)], held.at[pl.ds(s, tile)], sems.at[i])
        for i, s in enumerate(starts)
    ]
    copies[0].start()
    copies[1].start()
    for i, s in enumerate(starts):
        copies[i].wait()
        if i + 2 < len(copies):
            copies[i + 2].start()
        block, t = i // parts, i % parts
        value = jnp.dot(held[pl.ds(s, tile), :], test[...], preferred_element_type=F32)
        if block < 3:
            remote[block, t * tile : (t + 1) * tile, :] = value
        else:
            own[t * tile : (t + 1) * tile, :] = value
        if block < 3 and t == parts - 1:
            remote[block, 0:quarter, :], remote[block, quarter:, :] = scaled(
                remote[block, 0:quarter, :]
            )


def combine_kernel(own, a, b, c, out):
    rows = own.shape[0]
    total = own[...] + unscaled(a) + unscaled(b) + unscaled(c)
    out[0:rows, :], out[rows:, :] = scaled(total)


def product_kernel(me, slab, p0, p1, p2, p3, pieces, gram, sketch, flipped, product):
    quarter = p0.shape[0] - TAIL
    for shift, piece in enumerate((p0, p1, p2, p3)):
        start = pl.multiple_of(lax.rem(me[0] + Y - shift, Y) * quarter, 16)
        value = unscaled(piece)
        high = value.astype(BF16)
        sketch[pl.ds(start, quarter), 0:128] = high
        sketch[pl.ds(start, quarter), 128:256] = (value - high.astype(F32)).astype(BF16)
    flipped[...] = sketch[...].T
    full = jnp.dot(flipped[...], sketch[...], preferred_element_type=F32)
    full = full[0:128] + full[128:256]
    gram[...] = full[:, 0:128] + full[:, 128:256]
    product[...] = jnp.dot(flipped[0:128, :], slab[...], preferred_element_type=F32)
    for j in range(16):
        block = product[:, 128 * j : 128 * (j + 1)].T
        for i in range(4):
            r = 4 * j + i
            z, x, c = r // (X * C), (r // C) % X, r % C
            place = lax.rem(x + X - me[2], X) * Z + lax.rem(z + Z - me[1], Z)
            other = lax.rem(c + me[3], C)
            pieces[other, pl.ds(pl.multiple_of(place * 32, 32), 32), :] = block[32 * i : 32 * i + 32]


def inverse_rows(gram):
    lane = lax.broadcasted_iota(jnp.int32, (8, 128), 1)
    sub = lax.broadcasted_iota(jnp.int32, (8, 128), 0)
    work = [gram[8 * i : 8 * i + 8, :] for i in range(16)]
    out = []
    for b in range(16):
        c0 = 8 * b
        inside = (lane >= c0) & (lane < c0 + 8)
        panel = work[b]
        column = [jnp.broadcast_to(panel[:, c0 + c : c0 + c + 1], (8, 128)) for c in range(8)]
        panel = jnp.where(inside, (lane - c0 == sub).astype(F32), panel)
        root, upper, row = [], {}, []
        scale = jnp.zeros((8, 128), F32)
        for k in range(8):
            pivot = jnp.broadcast_to(column[k][k : k + 1, :], (8, 128))
            r = lax.rsqrt(pivot)
            r = r * (1.5 - 0.5 * pivot * r * r)
            root.append(r)
            row.append(jnp.broadcast_to(panel[k : k + 1, :], (8, 128)) * r)
            scale = jnp.where(sub == k, r, scale)
            if k < 7:
                m = jnp.where(sub > k, column[k] * r, 0.0)
                panel = panel - m * row[k]
                for c in range(k + 1, 8):
                    upper[k, c] = jnp.broadcast_to(column[c][k : k + 1, :], (8, 128)) * r
                    column[c] = column[c] - m * upper[k, c]
        out.append(jnp.where(lane <= sub + c0, panel * scale, 0.0))
        for i in range(b + 1, 16):
            left = [jnp.broadcast_to(work[i][:, c0 + c : c0 + c + 1], (8, 128)) for c in range(8)]
            rest = jnp.where(inside, 0.0, work[i])
            for k in range(8):
                m = left[k] * root[k]
                for c in range(k + 1, 8):
                    left[c] = left[c] - m * upper[k, c]
                rest = rest - m * row[k]
            work[i] = rest
    return out


def finish_kernel(total_rows, gram, sketch, product, basis, projected, factor, weights):
    rows = inverse_rows(gram[...] * (1.0 / total_rows))
    for i, value in enumerate(rows):
        factor[8 * i : 8 * i + 8, :] = value
    value = factor[...]
    high = value.astype(BF16)
    low = (value - high.astype(F32)).astype(BF16)
    for k in range(2):
        weights[0:128, 128 * k : 128 * k + 128] = high
        weights[128:256, 128 * k : 128 * k + 128] = low
    dims = (((1,), (1,)), ((), ()))
    step = sketch.shape[0] // 4
    for i in range(4):
        at = slice(step * i, step * (i + 1))
        wide = lax.dot_general(sketch[at, :], weights[...], dims, preferred_element_type=F32)
        basis[at, :] = (wide[:, 0:128] + wide[:, 128:256]).astype(BF16)
    projected[...] = lax.dot_general(
        product[...], value, dims, precision=lax.Precision.HIGHEST, preferred_element_type=F32
    ) * (1.0 / total_rows**0.5)


def shape(rows, columns, kind):
    return jax.ShapeDtypeStruct((rows, columns), kind)


def body(slab, test_matrix):
    rows, columns = slab.shape
    width = test_matrix.shape[1]
    total_rows = rows * lax.axis_size("row")
    quarter = rows // Y
    block = quarter + TAIL
    row = lax.axis_index("row")
    me_c = row % C
    me = jnp.stack([lax.axis_index("col"), row // (X * C), (row // C) % X, me_c]).astype(jnp.int32)

    remote, own, held = pl.pallas_call(
        sketch_kernel,
        name="sketch",
        out_shape=(
            jax.ShapeDtypeStruct((3, block, width), F32),
            shape(quarter, width, F32),
            shape(rows, columns, BF16),
        ),
        in_specs=[SMEM, ANY, VMEM],
        out_specs=(VMEM, VMEM, VMEM),
        scratch_shapes=[pltpu.SemaphoreType.DMA((8,))],
        compiler_params=pltpu.CompilerParams(vmem_limit_bytes=40 * MIB),
    )(me, slab, test_matrix)

    received = [
        col_shift(remote[i].astype(F16), dy).astype(F32) for i, dy in enumerate((2, 1, 3))
    ]
    own = pl.pallas_call(
        combine_kernel,
        name="combine",
        out_shape=shape(block, width, F32),
        in_specs=[VMEM] * 4,
        out_specs=VMEM,
    )(own, *received)

    own = own.astype(F16)
    gathered = [own] + [col_shift(own, dy) for dy in (1, 2, 3)]
    pieces, gram, sketch = pl.pallas_call(
        product_kernel,
        name="product",
        out_shape=(
            jax.ShapeDtypeStruct((2, columns // 2, width), F32),
            shape(width, width, F32),
            shape(rows, 2 * width, BF16),
        ),
        in_specs=[SMEM, VMEM] + [VMEM] * 4,
        out_specs=(VMEM, VMEM, VMEM),
        scratch_shapes=[pltpu.VMEM((2 * width, rows), BF16), pltpu.VMEM((width, columns), F32)],
        compiler_params=pltpu.CompilerParams(vmem_limit_bytes=40 * MIB),
    )(me, held, *[piece.astype(F32) for piece in gathered])

    half = width // C

    def half_of(index):
        return lax.dynamic_slice_in_dim(gram, index * half, half, 0)

    def with_gram(a, g):
        return jnp.concatenate([a, g], 0)

    got = row_shift(with_gram(pieces[1], half_of(1 - me_c)), 0, 0, 1)
    mine = pieces[0] + got[:-half]
    part = half_of(me_c) + got[-half:]

    wide = mine.shape[0] // X
    total, gsum = mine[:wide], part
    for dx in (2, 1, 3):
        got = row_shift(with_gram(mine[dx * wide : (dx + 1) * wide], part), 0, dx, 0)
        total, gsum = total + got[:wide], gsum + got[wide:]

    thin = wide // Z
    chunk = [total[thin * i : thin * (i + 1)] for i in range(Z)]
    back = row_shift(jnp.concatenate(chunk[4:7] + [gsum], 0), -3, 0, 0)
    ahead = row_shift(jnp.concatenate(chunk[2:4] + [gsum], 0), 2, 0, 0)
    before = chunk[7] + back[:thin]
    centre = chunk[0] + back[thin : 2 * thin] + ahead[:thin]
    after = chunk[1] + back[2 * thin : 3 * thin] + ahead[thin : 2 * thin]
    gsum = gsum + back[3 * thin :]
    gall = gsum + ahead[2 * thin :]
    left = row_shift(with_gram(before, gsum), -1, 0, 0)
    right = row_shift(with_gram(after, gall), 1, 0, 0)
    product = centre + left[:thin] + right[:thin]
    gsum = gall + left[thin:] + right[thin:]
    other = row_shift(gsum, 0, 0, 1)
    first = me_c == 0
    gram = with_gram(jnp.where(first, gsum, other), jnp.where(first, other, gsum))

    def finish(*refs):
        finish_kernel(total_rows, *refs)

    return pl.pallas_call(
        finish,
        name="finish",
        out_shape=(shape(rows, width, BF16), shape(thin, width, F32)),
        scratch_shapes=[pltpu.VMEM((width, width), F32), pltpu.VMEM((2 * width, 2 * width), BF16)],
        compiler_params=pltpu.CompilerParams(vmem_limit_bytes=40 * MIB),
    )(gram, sketch, product)


def solution(mesh):
    placed = (P("row", "col"), P("col", None))
    return jax.shard_map(
        body,
        mesh=mesh,
        in_specs=placed,
        out_specs=(P("row", None), P(("col", "row"), None)),
        check_vma=False,
    )
```
